256 devices in a mesh: dp: 32 (over z, x), head: 4 (over y), grp: 2 (over core).
Axes of the slice: x: 4, y: 4, z: 8, core: 2. Of those that a mesh axis runs over, the one named last changes fastest.
Arguments:
- attn_partial: bfloat16 [2, 4, 4096, 3584], P(None, 'head', ('dp', 'grp')), may hold values from -4 to 4
- residual: bfloat16 [2, 4096, 3584], P(None, ('dp', 'grp')), may hold values from -13 to 13
- norm_gain: float32 [3584], replicated, may hold values from 0.5 to 1.5
- expert_ids: int32 [2, 4096, 8], P(None, ('dp', 'grp')), may hold values from 0 to 127, all different within a row; in each aligned block of 16 rows (0 to 15, 16 to 31, ..., all dimensions but the last counted through in order) at most 2 rows name the same one
- gate_weights: float32 [2, 4096, 8], P(None, ('dp', 'grp')), may hold values from 0.05 to 0.5
- w_gate: bfloat16 [128, 3584, 1024], P(('dp', 'grp'), None, 'head'), may hold values from -0.09375 to 0.09375
- w_up: bfloat16 [128, 3584, 1024], P(('dp', 'grp'), None, 'head'), may hold values from -0.09375 to 0.09375
- w_down: bfloat16 [128, 1024, 3584], P(('dp', 'grp'), 'head'), may hold values from -0.1875 to 0.1875
Outputs:
- layer_out: bfloat16 [2, 4096, 3584], P(None, ('dp', 'grp', 'head'))
The draws below stay inside these ranges and needn't reach their ends.
Inputs may be any that keep to these rules, and one draw needn't show every extreme that they name: `expert_ids`: each token names 8 different experts; within the 16 tokens of one device (aligned blocks of 16 tokens of a micro-batch) no expert is named by more than 2 tokens, a bound that some block reaches.
All inputs are finite; a program needn't handle non-finite values.
Results may differ from the reference program's by a relative error of at most 0.014.
Values may be sent and summed in bfloat16 or wider, within the bound.
No kernel may reach another device: no remote copies, remote signals or barrier semaphores. Data moves between devices by JAX's collectives and lax.ppermute only.
A program may use at most 128 MiB of HBM per device.

```python
import math
import jax
import jax.numpy as jnp
import numpy as np
from jax import lax

D = 3584
EXPERT_HID = 1024
TOPK = 8
MB = 2
ROWS = 16
EXPERTS = 128
TOKENS = 4096
CAP = 2
N_HEAD = 4


def draw_residual(key, part):
    key = jax.random.fold_in(key, 11)
    first, second = jax.random.split(key, 2)
    scales = 0.3 * jnp.exp(jax.random.uniform(second, (MB, TOKENS, 1), jnp.float32) * jnp.log(10.0))
    values = jax.random.truncated_normal(first, -4.0, 4.0, (MB, TOKENS, D), jnp.float32) * scales
    return values.astype(jnp.bfloat16)


def block_scale(stream_key, shape, cuts, smallest, largest):
    factor_of, own = 1.0, jax.random.fold_in(stream_key, 6)
    for dim, shards_of in cuts:
        steps = jnp.exp(jax.random.uniform(jax.random.fold_in(own, dim), (shards_of,), jnp.float32, smallest / len(cuts), largest / len(cuts)))
        factor_of = factor_of * jnp.repeat(steps, shape[dim] // shards_of).reshape([-1 if axis == dim else 1 for axis in range(len(shape))])
    return factor_of


def assign_block(rng, own, number, rows, amount, top, most, skew):
    order = jax.random.permutation(rng, amount)
    heavy_load, usual = shares(amount, rows * top, most, skew, True), shares(amount, rows * top, most, skew, False)
    places = jnp.arange(amount)

    def named(lengths, offset_by):
        used = int((lengths > 0).sum())
        fixed = max(1, used // 4)
        moved = fixed + (places - fixed + offset_by * (used - fixed)) % max(1, amount - fixed)
        return jnp.zeros((amount,), jnp.int32).at[order[jnp.where(places < fixed, places, moved)]].set(jnp.asarray(lengths, jnp.int32))

    lengths = jnp.where(number % 4 == 0, named(heavy_load, number // 4), named(usual, number - number // 4 - 1))
    mixed = jax.random.permutation(jax.random.fold_in(own, 3), amount)
    source_of, taker = mixed[0:amount // 2 * 2:2], mixed[1:amount // 2 * 2:2]
    room = jnp.minimum(lengths[source_of] - 1, most - lengths[taker]) // 2
    room = jnp.where((source_of == order[0]) | (taker == order[0]) | (lengths[taker] == 0), 0, jnp.maximum(room, 0))
    moved = jax.random.randint(jax.random.fold_in(own, 4), (amount // 2,), 0, 1 << 20) % (room + 1)
    lengths = lengths.at[source_of].add(-moved).at[taker].add(moved)
    labels = jnp.searchsorted(jnp.cumsum(lengths), jnp.arange(rows * top), side="right").astype(jnp.int32)
    grid = labels.reshape(top, rows).T
    grid = grid[jax.random.permutation(jax.random.fold_in(own, 1), rows)]
    offset_by = jax.random.randint(jax.random.fold_in(own, 2), (rows, 1), 0, top)
    return jnp.take_along_axis(grid, (jnp.arange(top)[None, :] + offset_by) % top, axis=1)


def shares(count, total, limit, lean, full):
    portions = [(1 << 20) // math.isqrt(rank ** lean) + 1 for rank in range(1, count + 1)]
    largest = limit if full else min(limit, max(-(-total // count), total * portions[0] // sum(portions)))
    least = 1 if total - largest >= count - 1 else 0
    given, surplus = [largest] + [least] * (count - 1), total - largest - least * (count - 1)
    while surplus > 0:
        free = [i for i in range(1, count) if given[i] < largest] or [i for i in range(1, count) if given[i] < limit]
        whole, left = sum([portions[i] for i in free]), surplus
        for i in free:
            addition = min(limit - given[i], max(1, left * portions[i] // whole), surplus)
            given[i] = given[i] + addition
            surplus = surplus - addition
    return np.array(given)


def centred(rng, dims, deviation, reach, shards=(), kind=jnp.bfloat16):
    entries = jax.random.normal(rng, dims, jnp.float32) * deviation
    if len(shards) > 0:
        entries = block_scale(rng, dims, shards, -0.22, 0.18) * entries
    return jnp.clip(entries, min=-reach, max=reach).astype(kind)


def setup_inputs(seed: int = 0) -> dict:
    key_of = jax.random.split(jax.random.key(seed), 9)
    attn_partial = centred(key_of[0], (MB, N_HEAD, TOKENS, D), 0.25, 4.0, ((1, 4), (2, 64)))
    residual = draw_residual(jax.random.fold_in(key_of[8], 71), 0)
    norm_gain = jnp.clip(1.0 + 0.1 * jax.random.normal(key_of[2], (D,), jnp.float32), 0.5, 1.5)
    expert_ids_keys = jax.random.split(jax.random.fold_in(key_of[3], 1), MB * TOKENS // ROWS)
    expert_ids_turns = jax.random.permutation(jax.random.fold_in(key_of[3], 3), MB * TOKENS // ROWS)
    expert_ids = jax.vmap(lambda own, number: assign_block(jax.random.fold_in(key_of[3], 2), own, number, ROWS, EXPERTS, TOPK, CAP, 2))(expert_ids_keys, expert_ids_turns).reshape((MB, TOKENS, TOPK))
    gate_weights = jnp.clip(0.05 + 0.45 * jax.random.uniform(key_of[4], (MB, TOKENS, TOPK), jnp.float32) ** block_scale(key_of[4], (MB, TOKENS, TOPK), ((1, 64),), -0.2, 0.2), 0.05, 0.5)
    w_gate = centred(key_of[5], (EXPERTS, D, EXPERT_HID), D ** -0.5, 0.09375, ((0, 64), (2, 4)))
    w_up = centred(key_of[6], (EXPERTS, D, EXPERT_HID), D ** -0.5, 0.09375, ((0, 64), (2, 4)))
    w_down = centred(key_of[7], (EXPERTS, EXPERT_HID, D), EXPERT_HID ** -0.5, 0.1875, ((0, 64), (1, 4)))
    return dict(attn_partial=attn_partial, residual=residual, norm_gain=norm_gain, expert_ids=expert_ids, gate_weights=gate_weights, w_gate=w_gate, w_up=w_up, w_down=w_down)


def normalize(stream, norm_gain):
    values = stream.astype(jnp.float32)
    factor = lax.rsqrt(lax.optimization_barrier(jnp.mean(values * values, axis=-1, keepdims=True)) + 1e-06)
    return (values * factor * norm_gain).astype(jnp.bfloat16)

def reference(attn_partial, residual, norm_gain, expert_ids, gate_weights, w_gate, w_up, w_down):
    stream = (residual.astype(jnp.float32) + lax.optimization_barrier(jnp.sum(attn_partial.astype(jnp.float32), axis=1))).astype(jnp.bfloat16)
    normed = normalize(stream, norm_gain)
    row_total = MB * TOKENS
    block_total = row_total // ROWS
    inputs = normed.reshape(row_total, D)
    flat_ids = expert_ids.reshape(-1).astype(jnp.int32)
    flat_gates = gate_weights.reshape(-1)
    route_count = flat_ids.shape[0]
    onehot = (flat_ids[:, None] == jnp.arange(EXPERTS, dtype=jnp.int32)[None, :]).astype(jnp.int32)
    stacked = onehot.reshape(block_total, ROWS * TOPK, EXPERTS)
    earlier = (jnp.cumsum(stacked, axis=1) - stacked).reshape(route_count, EXPERTS)
    slot_of = lax.optimization_barrier(jnp.sum(earlier * onehot, axis=1)).astype(jnp.int32)
    block_of = jnp.arange(route_count, dtype=jnp.int32) // (ROWS * TOPK)
    position = (flat_ids * block_total + block_of) * CAP + slot_of
    slot_total = EXPERTS * block_total * CAP
    token_of = jnp.zeros((slot_total,), jnp.int32).at[position].set(jnp.arange(route_count, dtype=jnp.int32) // TOPK)
    weight_of = jnp.zeros((slot_total,), jnp.float32).at[position].set(flat_gates)
    token_of = token_of.reshape(EXPERTS, block_total * CAP)
    weight_of = weight_of.reshape(EXPERTS, block_total * CAP)

    def expert_step(accum, pieces):
        tokens_e, weights_e, gate_e, up_e, down_e = pieces
        chosen = inputs[tokens_e]
        gate_pre = jnp.dot(chosen, gate_e, preferred_element_type=jnp.float32)
        upper = jnp.dot(chosen, up_e, preferred_element_type=jnp.float32)
        active = (jax.nn.silu(gate_pre) * upper).astype(jnp.bfloat16)
        quarters = active.reshape(-1, N_HEAD, EXPERT_HID // N_HEAD).astype(jnp.float32)
        down_parts = down_e.reshape(N_HEAD, EXPERT_HID // N_HEAD, D).astype(jnp.float32)
        partial_out = jnp.einsum('mqh,qhd->mqd', quarters, down_parts).astype(jnp.bfloat16)
        expert_out = lax.optimization_barrier(jnp.sum(partial_out.astype(jnp.float32), axis=1)).astype(jnp.bfloat16)
        accum = accum.at[tokens_e].add(weights_e[:, None] * expert_out.astype(jnp.float32))
        return (accum, None)
    accum, _ = lax.scan(expert_step, jnp.zeros((row_total, D), jnp.float32), (token_of, weight_of, w_gate, w_up, w_down))
    layer_out = (stream.reshape(row_total, D).astype(jnp.float32) + accum).astype(jnp.bfloat16)
    return layer_out.reshape(MB, TOKENS, D)
```

```python
import jax
import jax.numpy as jnp
from jax import lax
from jax.sharding import Mesh, PartitionSpec as P

NZ, NX, NY, NG = 8, 4, 4, 2
SLOTS = 2


def normalize(stream, norm_gain):
    values = stream.astype(jnp.float32)
    factor = lax.rsqrt(jnp.mean(values * values, axis=-1, keepdims=True) + 1e-06)
    return (values * factor * norm_gain).astype(jnp.bfloat16)


def yg_perm(first, second):
    return [(y * NG + g, (first(y) if g == 0 else second(y)) * NG + g) for y in range(NY) for g in range(NG)]


def mirror(y):
    return NY - 1 - y


def flip(y):
    return y ^ 1


SWAP = yg_perm(mirror, flip)
PAIR = yg_perm(flip, mirror)
CORES = [(0, 1), (1, 0)]


def swap(value):
    return lax.ppermute(value, ("y", "g"), SWAP)


def pair(value):
    return lax.ppermute(value, ("y", "g"), PAIR)


def turn(value, step):
    return lax.ppermute(value, "x", [(i, (i + step) % NX) for i in range(NX)])


def tables(ids, gates, rows, z, x, g):
    tokens, top = ids.shape
    blocks = tokens // rows
    slots = NX * 2 * blocks * SLOTS
    slot = jnp.arange(slots, dtype=jnp.int32)[None, :]
    token = jnp.arange(tokens, dtype=jnp.int32)[:, None]
    which = slot // (blocks * SLOTS)
    expert = (z * NX + (x + which // 2) % NX) * (2 * NG) + g * 2 + which % 2
    same_block = (slot // SLOTS) % blocks == token // rows
    member = jnp.zeros((tokens, slots), jnp.float32)
    weight = jnp.zeros((tokens, slots), jnp.float32)
    for k in range(top):
        hit = (ids[:, k : k + 1] == expert) & same_block
        member = jnp.where(hit, 1.0, member)
        weight = jnp.where(hit, gates[:, k : k + 1], weight)
    other = jnp.arange(tokens, dtype=jnp.int32)[None, :]
    before = ((other < token) & (other // rows == token // rows)).astype(jnp.bfloat16)
    earlier = jnp.dot(before, member.astype(jnp.bfloat16), preferred_element_type=jnp.float32)
    taken = (member > 0.5) & (earlier.astype(jnp.int32) == slot % SLOTS)
    return taken.astype(jnp.bfloat16), jnp.where(taken, weight, 0.0)


def per_device(attn_partial, residual, norm_gain, expert_ids, gate_weights, w_gate, w_up, w_down):
    micros = residual.shape[0]
    rows = residual.shape[1] // NY
    width = residual.shape[2]
    z, y, g = lax.axis_index("z"), lax.axis_index("y"), lax.axis_index("g")
    x = lax.axis_index("x")
    keep = jnp.where(g == 0, y // 2, jnp.where((y == 1) | (y == 2), 0, 1))

    def mine(value):
        return lax.dynamic_slice_in_dim(value, y * rows, rows, 1)

    outgoing = attn_partial[:, 0].reshape(micros, NY, rows, width).transpose(1, 0, 2, 3)
    parts = lax.all_to_all(outgoing, "y", 0, 0, tiled=True)

    packed = jnp.concatenate([mine(expert_ids).astype(jnp.float32), mine(gate_weights)], axis=-1)
    both = jnp.stack([packed, lax.ppermute(packed, "g", CORES)], axis=1)
    line = lax.all_gather(both, "z", axis=2)
    line = line.reshape(micros, -1, line.shape[-1])
    top = expert_ids.shape[-1]

    summed = jnp.sum(parts.astype(jnp.float32), axis=0)
    stream = (mine(residual).astype(jnp.float32) + summed).astype(jnp.bfloat16)
    normed = normalize(stream, norm_gain)

    def give(value):
        return lax.dynamic_index_in_dim(value, 1 - keep, 0, keepdims=False)

    def hold(value):
        return lax.dynamic_index_in_dim(value, keep, 0, keepdims=False)

    kept = [hold(w) for w in (w_gate, w_up, w_down)]
    got = [swap(give(w)) for w in (w_gate, w_up, w_down)]

    def experts(value):
        total = None
        for gate, up, down in (kept, got):
            gate_pre = jnp.dot(value, gate, preferred_element_type=jnp.float32)
            upper = jnp.dot(value, up, preferred_element_type=jnp.float32)
            active = (jax.nn.silu(gate_pre) * upper).astype(jnp.bfloat16)
            part = jnp.dot(active, down, preferred_element_type=jnp.float32)
            total = part if total is None else total + part
        return total

    tokens_z = lax.all_gather(normed, "z", axis=1)
    tokens_z = tokens_z.reshape(micros, NZ * rows, width)
    tokens_other = lax.ppermute(tokens_z, "g", CORES)
    back = []
    for m in range(micros):
        tokens = jnp.concatenate([tokens_z[m], tokens_other[m]], axis=0)
        chooser, mixing = tables(
            line[m, :, :top].astype(jnp.int32), line[m, :, top:], rows, z, x, g
        )
        routed = jnp.einsum("ts,td->sd", chooser, tokens, preferred_element_type=jnp.float32)
        routed = routed.astype(jnp.bfloat16)
        chunk = routed.shape[0] // NX
        routed = routed.reshape(NX, 2, chunk // 2, width)
        arrived = []
        for step in range(NX):
            arrived.append(routed[step] if step == 0 else turn(routed[step], step))
        arrived = jnp.stack(arrived, axis=1)
        stay = hold(arrived).reshape(-1, width)
        leave = give(arrived).reshape(-1, width)
        mine_rows = jnp.concatenate([stay, swap(leave)], axis=0)
        pair_rows = pair(mine_rows)
        pair_out = experts(pair_rows).astype(jnp.bfloat16)
        mine_out = experts(mine_rows)
        full = (mine_out + pair(pair_out).astype(jnp.float32)).astype(jnp.bfloat16)
        half = full.shape[0] // 2
        own, away = full[:half], swap(full[half:])
        first = jnp.where(keep == 0, own, away).reshape(NX, -1, width)
        second = jnp.where(keep == 0, away, own).reshape(NX, -1, width)
        answers = []
        for step in range(NX):
            piece = jnp.concatenate([first[step], second[step]], axis=0)
            answers.append(piece if step == 0 else turn(piece, -step))
        ordered = jnp.concatenate(answers, axis=0)
        coarse = mixing.astype(jnp.bfloat16)
        fine = (mixing - coarse.astype(jnp.float32)).astype(jnp.bfloat16)
        total = jnp.dot(coarse, ordered, preferred_element_type=jnp.float32) + jnp.dot(
            fine, ordered, preferred_element_type=jnp.float32
        )
        own_total, other_total = total[: NZ * rows], total[NZ * rows :]
        other_total = lax.ppermute(other_total.astype(jnp.bfloat16), "g", CORES)
        line_total = (own_total + other_total.astype(jnp.float32)).astype(jnp.bfloat16)
        back.append(line_total.reshape(NZ, rows, width))
    back = jnp.stack(back, axis=1)
    sums = lax.all_to_all(back, "z", 0, 0, tiled=True)
    layer = stream.astype(jnp.float32) + jnp.sum(sums.astype(jnp.float32), axis=0)
    return layer.astype(jnp.bfloat16)


def solution(mesh):
    fine = Mesh(mesh.devices.reshape(NZ, NX, NY, NG), ("z", "x", "y", "g"))
    owners = ("z", "x", "g")
    return jax.shard_map(
        per_device,
        mesh=fine,
        in_specs=(
            P(None, "y", owners, None),
            P(None, owners, None),
            P(),
            P(None, owners, None),
            P(None, owners, None),
            P(owners, None, "y"),
            P(owners, None, "y"),
            P(owners, "y", None),
        ),
        out_specs=P(None, ("z", "x", "g", "y"), None),
        check_vma=False,
    )
```

```python
import jax
import jax.numpy as jnp
from jax import lax
from jax.experimental import pallas as pl
from jax.experimental.pallas import tpu as pltpu
from jax.sharding import Mesh, PartitionSpec as P

NZ, NX, NY, NG = 8, 4, 4, 2
SLOTS = 2
CHUNKS = 2
LANES = 128


def normalize(stream, norm_gain):
    values = stream.astype(jnp.float32)
    factor = lax.rsqrt(jnp.mean(values * values, axis=-1, keepdims=True) + 1e-06)
    return (values * factor * norm_gain).astype(jnp.bfloat16)


def yg_perm(first, second):
    return [(y * NG + g, (first(y) if g == 0 else second(y)) * NG + g) for y in range(NY) for g in range(NG)]


def mirror(y):
    return NY - 1 - y


def flip(y):
    return y ^ 1


SWAP = yg_perm(mirror, flip)
PAIR = yg_perm(flip, mirror)
CORES = [(0, 1), (1, 0)]


def swap(value):
    return lax.ppermute(value, ("y", "g"), SWAP)


def pair(value):
    return lax.ppermute(value, ("y", "g"), PAIR)


def cores(value):
    return lax.ppermute(value, "g", CORES)


def turn(value, axis, size, step):
    return lax.ppermute(value, axis, [(i, (i + step) % size) for i in range(size)])


def along(value, step):
    pairs = [(z * NG + g, (z + (step if g == 0 else -step)) % NZ * NG + g) for z in range(NZ) for g in range(NG)]
    return lax.ppermute(value, ("z", "g"), pairs)


def tables(ids, gates, rows, z, x, g, keep):
    tokens, top = ids.shape
    blocks = tokens // rows
    slots = NX * 2 * blocks * SLOTS
    slot = jnp.arange(slots, dtype=jnp.int32)[None, :]
    token = jnp.arange(tokens, dtype=jnp.int32)[:, None]
    which = slot // (blocks * SLOTS)
    local = jnp.where(which % 2 == 0, keep, 1 - keep)
    expert = (z * NX + (x + which // 2) % NX) * (2 * NG) + g * 2 + local
    same_block = (slot // SLOTS) % blocks == token // rows
    member = jnp.zeros((tokens, slots), jnp.float32)
    weight = jnp.zeros((tokens, slots), jnp.float32)
    for k in range(top):
        hit = (ids[:, k : k + 1] == expert) & same_block
        member = jnp.where(hit, 1.0, member)
        weight = jnp.where(hit, gates[:, k : k + 1], weight)
    other = jnp.arange(tokens, dtype=jnp.int32)[None, :]
    before = ((other < token) & (other // rows == token // rows)).astype(jnp.bfloat16)
    earlier = jnp.dot(before, member.astype(jnp.bfloat16), preferred_element_type=jnp.float32)
    taken = (member > 0.5) & (earlier.astype(jnp.int32) == slot % SLOTS)
    weight = jnp.where(taken, weight, 0.0)
    coarse = weight.astype(jnp.bfloat16)
    fine = (weight - coarse.astype(jnp.float32)).astype(jnp.bfloat16)
    return taken.astype(jnp.bfloat16), coarse, fine


def expert_kernel(keep_ref, a_ref, b_ref, gk, uk, got_ref, dk, dg, oa_ref, ob_ref, act):
    step = pl.program_id(0)
    half = a_ref.shape[0]
    hid = gk.shape[1]

    @pl.when(step == 0)
    def _():
        rows = jnp.concatenate([a_ref[...], b_ref[...]], axis=0)
        for n, (up_to, by) in enumerate(((gk, uk), (got_ref.at[0], got_ref.at[1]))):
            gate = jnp.dot(rows, up_to[...], preferred_element_type=jnp.float32)
            upper = jnp.dot(rows, by[...], preferred_element_type=jnp.float32)
            active = gate / (1.0 + jnp.exp(-gate)) * upper
            act[:, n * hid : (n + 1) * hid] = active.astype(jnp.bfloat16)

    @pl.when(step > 0)
    def _():
        out = jnp.dot(act[:, :hid], dk[...], preferred_element_type=jnp.float32)
        out += jnp.dot(act[:, hid:], dg[...], preferred_element_type=jnp.float32)
        out = out.astype(jnp.bfloat16)
        oa_ref[...] = out[:half]
        ob_ref[...] = out[half:]


def experts(keep, a, b, kept, got):
    half, width = a.shape
    hid = got[1].shape[0]
    wide = width // CHUNKS

    def late(i):
        return jnp.maximum(i - 1, 0)

    rows_spec = pl.BlockSpec((half, width), lambda i, keep: (0, 0))
    kept_up = pl.BlockSpec((None, width, hid), lambda i, keep: (keep[0], 0, 0))
    got_up = pl.BlockSpec((2, width, hid), lambda i, keep: (0, 0, 0))
    kept_down = pl.BlockSpec((None, hid, wide), lambda i, keep: (keep[0], 0, late(i)))
    got_down = pl.BlockSpec((hid, wide), lambda i, keep: (0, late(i)))
    out_spec = pl.BlockSpec((half, wide), lambda i, keep: (0, late(i)))
    return pl.pallas_call(
        expert_kernel,
        out_shape=[jax.ShapeDtypeStruct((half, width), jnp.bfloat16)] * 2,
        grid_spec=pltpu.PrefetchScalarGridSpec(
            num_scalar_prefetch=1,
            grid=(1 + CHUNKS,),
            in_specs=[rows_spec, rows_spec, kept_up, kept_up, got_up, kept_down, got_down],
            out_specs=[out_spec, out_spec],
            scratch_shapes=[pltpu.VMEM((2 * half, 2 * hid), jnp.bfloat16)],
        ),
        compiler_params=pltpu.CompilerParams(
            dimension_semantics=("arbitrary",), vmem_limit_bytes=36 * 1024 * 1024
        ),
        cost_estimate=pl.CostEstimate(
            flops=2 * 2 * half * width * hid * 6,
            bytes_accessed=2 * (6 * hid * width + 4 * half * width),
            transcendentals=2 * half * 2 * hid,
        ),
    )(keep.reshape(1), a, b, kept[0], kept[1], got[0], kept[2], got[1])


def tie_kernel(value_ref, after_ref, out_ref):
    del value_ref, after_ref, out_ref


def tie(value, after):
    return pl.pallas_call(
        tie_kernel,
        out_shape=jax.ShapeDtypeStruct(value.shape, value.dtype),
        in_specs=[pl.BlockSpec(memory_space=pl.ANY)] * 2,
        out_specs=pl.BlockSpec(memory_space=pl.ANY),
        input_output_aliases={0: 0},
        cost_estimate=pl.CostEstimate(flops=0, bytes_accessed=0, transcendentals=0),
    )(value, after)


def per_device(attn_partial, residual, norm_gain, expert_ids, gate_weights, w_gate, w_up, w_down):
    micros = residual.shape[0]
    rows = residual.shape[1] // NY
    width = residual.shape[2]
    top = expert_ids.shape[-1]
    z, x, y, g = (lax.axis_index(name) for name in ("z", "x", "y", "g"))
    keep = jnp.where(g == 0, y // 2, jnp.where((y == 1) | (y == 2), 0, 1)).astype(jnp.int32)

    def part_of(value, who):
        return lax.dynamic_slice_in_dim(value, who * rows, rows, value.ndim - 2)

    sums = part_of(attn_partial[:, 0], y).astype(jnp.float32)
    for step in range(1, NY):
        piece = part_of(attn_partial[:, 0], (y + step) % NY)
        sums = sums + turn(piece, "y", NY, step).astype(jnp.float32)
    stream = (part_of(residual, y).astype(jnp.float32) + sums).astype(jnp.bfloat16)
    normed = normalize(stream, norm_gain)

    def give(value):
        return lax.dynamic_index_in_dim(value, 1 - keep, 0, keepdims=False)

    kept = (w_gate, w_up, w_down)
    got_up = swap(tie(jnp.stack([give(w_gate), give(w_up)]), normed))
    got_down = swap(tie(give(w_down), got_up))
    got = (got_up, got_down)

    left, digits = part_of(gate_weights, y), []
    for _ in range(3):
        digits.append(left.astype(jnp.bfloat16))
        left = left - digits[-1].astype(jnp.float32)
    fields = [part_of(expert_ids, y).astype(jnp.bfloat16), *digits]
    fields.append(jnp.zeros((micros, rows, LANES - 4 * top), jnp.bfloat16))
    sent = jnp.concatenate([normed, *fields], axis=-1)
    both = jnp.concatenate([sent, cores(sent)], axis=1)
    line = [sent]
    for step in range(1, NZ // 2):
        line.append(along(both, step))
    line.append(along(sent, NZ // 2))
    line = tie(jnp.concatenate(line, axis=1), got_up)
    across = cores(line)

    arrivals, mixings = [], []
    for m in range(micros):
        tokens = jnp.concatenate([line[m], across[m]], axis=0)
        fields = tokens[:, width:].astype(jnp.float32)
        gates = fields[:, top : 2 * top] + fields[:, 2 * top : 3 * top] + fields[:, 3 * top : 4 * top]
        chooser, *mixing = tables(fields[:, :top].astype(jnp.int32), gates, rows, z, x, g, keep)
        mixings.append(mixing)
        routed = jnp.einsum("ts,td->sd", chooser, tokens[:, :width], preferred_element_type=jnp.float32)
        routed = routed.astype(jnp.bfloat16).reshape(NX, -1, width)
        arrived = [routed[step] if step == 0 else turn(routed[step], "x", NX, step) for step in range(NX)]
        arrivals.append(jnp.stack(arrived))

    results = []
    last = None
    for m in range(micros):
        arrived = arrivals[m]
        half = arrived.shape[1] // 2
        stay = arrived[:, :half].reshape(-1, width)
        leave = arrived[:, half:].reshape(-1, width)
        if m == 0:
            leave = tie(leave, got_down)
        came = swap(leave)
        if m == 0:
            pair_stay, pair_came = pair(stay), pair(came)
            last = pair_came
        else:
            pair_stay, pair_came = pair(tie(stay, last)), pair(tie(came, last))
        mine_stay, mine_came = experts(keep, stay, came, kept, got)
        pair_stay, pair_came = experts(keep, pair_stay, pair_came, kept, got)
        away = (mine_came.astype(jnp.float32) + pair(pair_came).astype(jnp.float32)).astype(jnp.bfloat16)
        away = swap(away)
        here = (mine_stay.astype(jnp.float32) + pair(pair_stay).astype(jnp.float32)).astype(jnp.bfloat16)
        answers = []
        for step in range(NX):
            span = slice(step * half, (step + 1) * half)
            piece = jnp.concatenate([here[span], away[span]], axis=0)
            answers.append(piece if step == 0 else turn(piece, "x", NX, -step))
        ordered = jnp.concatenate(answers, axis=0)
        if m > 0:
            ordered = tie(ordered, results[-1])
        total = jnp.dot(mixings[m][0], ordered, preferred_element_type=jnp.float32) + jnp.dot(
            mixings[m][1], ordered, preferred_element_type=jnp.float32
        )
        count = NZ * rows
        other = cores(total[count:].astype(jnp.bfloat16))
        back = (total[:count] + other.astype(jnp.float32)).astype(jnp.bfloat16)
        layer = stream[m].astype(jnp.float32) + back[:rows].astype(jnp.float32)
        beside = jnp.zeros((rows, width), jnp.float32)
        for step in range(1, NZ // 2):
            first = (2 * step - 1) * rows
            came = along(back[first : first + 2 * rows], -step).astype(jnp.float32)
            layer, beside = layer + came[:rows], beside + came[rows:]
        layer = layer + along(back[count - rows :], NZ // 2).astype(jnp.float32)
        layer = layer + cores(beside.astype(jnp.bfloat16)).astype(jnp.float32)
        results.append(layer.astype(jnp.bfloat16))
    return jnp.stack(results)


def solution(mesh):
    fine = Mesh(mesh.devices.reshape(NZ, NX, NY, NG), ("z", "x", "y", "g"))
    owners = ("z", "x", "g")
    return jax.shard_map(
        per_device,
        mesh=fine,
        in_specs=(
            P(None, "y", owners, None),
            P(None, owners, None),
            P(),
            P(None, owners, None),
            P(None, owners, None),
            P(owners, None, "y"),
            P(owners, None, "y"),
            P(owners, "y", None),
        ),
        out_specs=P(None, ("z", "x", "g", "y"), None),
        check_vma=False,
    )
```

```python
import jax
import jax.numpy as jnp
from jax import lax
from jax.experimental import pallas as pl
from jax.experimental.pallas import tpu as pltpu
from jax.sharding import Mesh, PartitionSpec as P

NZ, NX, NY, NG = 8, 4, 4, 2
SLOTS = 2
CHUNKS = 2
LANES = 128


def normalize(stream, norm_gain):
    values = stream.astype(jnp.float32)
    factor = lax.rsqrt(jnp.mean(values * values, axis=-1, keepdims=True) + 1e-06)
    return (values * factor * norm_gain).astype(jnp.bfloat16)


def yg_perm(first, second):
    return [(y * NG + g, (first(y) if g == 0 else second(y)) * NG + g) for y in range(NY) for g in range(NG)]


def mirror(y):
    return NY - 1 - y


def flip(y):
    return y ^ 1


SWAP = yg_perm(mirror, flip)
PAIR = yg_perm(flip, mirror)
CORES = [(0, 1), (1, 0)]


def swap(value):
    return lax.ppermute(value, ("y", "g"), SWAP)


def pair(value):
    return lax.ppermute(value, ("y", "g"), PAIR)


def cores(value):
    return lax.ppermute(value, "g", CORES)


def turn(value, axis, size, step):
    return lax.ppermute(value, axis, [(i, (i + step) % size) for i in range(size)])


def along(value, step):
    pairs = [(z * NG + g, (z + (step if g == 0 else -step)) % NZ * NG + g) for z in range(NZ) for g in range(NG)]
    return lax.ppermute(value, ("z", "g"), pairs)


def tables(ids, gates, rows, z, x, g, keep):
    tokens, top = ids.shape
    blocks = tokens // rows
    slots = NX * 2 * blocks * SLOTS
    slot = jnp.arange(slots, dtype=jnp.int32)[None, :]
    token = jnp.arange(tokens, dtype=jnp.int32)[:, None]
    which = slot // (blocks * SLOTS)
    local = jnp.where(which % 2 == 0, keep, 1 - keep)
    expert = (z * NX + (x + which // 2) % NX) * (2 * NG) + g * 2 + local
    same_block = (slot // SLOTS) % blocks == token // rows
    member = jnp.zeros((tokens, slots), jnp.float32)
    weight = jnp.zeros((tokens, slots), jnp.float32)
    for k in range(top):
        hit = (ids[:, k : k + 1] == expert) & same_block
        member = jnp.where(hit, 1.0, member)
        weight = jnp.where(hit, gates[:, k : k + 1], weight)
    other = jnp.arange(tokens, dtype=jnp.int32)[None, :]
    before = ((other < token) & (other // rows == token // rows)).astype(jnp.bfloat16)
    earlier = jnp.dot(before, member.astype(jnp.bfloat16), preferred_element_type=jnp.float32)
    taken = (member > 0.5) & (earlier.astype(jnp.int32) == slot % SLOTS)
    weight = jnp.where(taken, weight, 0.0)
    coarse = weight.astype(jnp.bfloat16)
    fine = (weight - coarse.astype(jnp.float32)).astype(jnp.bfloat16)
    return taken.astype(jnp.bfloat16), coarse, fine


def expert_kernel(keep_ref, a_ref, b_ref, gk, uk, got_ref, dk, dg, after_ref, oa_ref, ob_ref, act):
    del after_ref
    step = pl.program_id(0)
    half = a_ref.shape[0]
    hid = gk.shape[1]

    @pl.when(step == 0)
    def _():
        rows = jnp.concatenate([a_ref[...], b_ref[...]], axis=0)
        for n, (up_to, by) in enumerate(((gk, uk), (got_ref.at[0], got_ref.at[1]))):
            gate = jnp.dot(rows, up_to[...], preferred_element_type=jnp.float32)
            upper = jnp.dot(rows, by[...], preferred_element_type=jnp.float32)
            active = gate / (1.0 + jnp.exp(-gate)) * upper
            act[:, n * hid : (n + 1) * hid] = active.astype(jnp.bfloat16)

    @pl.when(step > 0)
    def _():
        out = jnp.dot(act[:, :hid], dk[...], preferred_element_type=jnp.float32)
        out += jnp.dot(act[:, hid:], dg[...], preferred_element_type=jnp.float32)
        out = out.astype(jnp.bfloat16)
        oa_ref[...] = out[:half]
        ob_ref[...] = out[half:]


def experts(keep, a, b, kept, got, after):
    half, width = a.shape
    hid = got[1].shape[0]
    wide = width // CHUNKS

    def late(i):
        return jnp.maximum(i - 1, 0)

    rows_spec = pl.BlockSpec((half, width), lambda i, keep: (0, 0))
    kept_up = pl.BlockSpec((None, width, hid), lambda i, keep: (keep[0], 0, 0))
    got_up = pl.BlockSpec((2, width, hid), lambda i, keep: (0, 0, 0))
    kept_down = pl.BlockSpec((None, hid, wide), lambda i, keep: (keep[0], 0, late(i)))
    got_down = pl.BlockSpec((hid, wide), lambda i, keep: (0, late(i)))
    out_spec = pl.BlockSpec((half, wide), lambda i, keep: (0, late(i)))
    return pl.pallas_call(
        expert_kernel,
        out_shape=[jax.ShapeDtypeStruct((half, width), jnp.bfloat16)] * 2,
        grid_spec=pltpu.PrefetchScalarGridSpec(
            num_scalar_prefetch=1,
            grid=(1 + CHUNKS,),
            in_specs=[rows_spec, rows_spec, kept_up, kept_up, got_up, kept_down, got_down, pl.BlockSpec(memory_space=pl.ANY)],
            out_specs=[out_spec, out_spec],
            scratch_shapes=[pltpu.VMEM((2 * half, 2 * hid), jnp.bfloat16)],
        ),
        compiler_params=pltpu.CompilerParams(
            dimension_semantics=("arbitrary",), vmem_limit_bytes=28 * 1024 * 1024
        ),
        cost_estimate=pl.CostEstimate(
            flops=2 * 2 * half * width * hid * 6,
            bytes_accessed=2 * (6 * hid * width + 4 * half * width),
            transcendentals=2 * half * 2 * hid,
        ),
    )(keep.reshape(1), a, b, kept[0], kept[1], got[0], kept[2], got[1], after)


def tie_kernel(value_ref, after_ref, out_ref):
    del value_ref, after_ref, out_ref


def tie(value, after):
    return pl.pallas_call(
        tie_kernel,
        out_shape=jax.ShapeDtypeStruct(value.shape, value.dtype),
        in_specs=[pl.BlockSpec(memory_space=pl.ANY)] * 2,
        out_specs=pl.BlockSpec(memory_space=pl.ANY),
        input_output_aliases={0: 0},
        cost_estimate=pl.CostEstimate(flops=0, bytes_accessed=0, transcendentals=0),
    )(value, after)


def per_device(attn_partial, residual, norm_gain, expert_ids, gate_weights, w_gate, w_up, w_down):
    micros = residual.shape[0]
    rows = residual.shape[1] // NY
    width = residual.shape[2]
    top = expert_ids.shape[-1]
    z, x, y, g = (lax.axis_index(name) for name in ("z", "x", "y", "g"))
    keep = jnp.where(g == 0, y // 2, jnp.where((y == 1) | (y == 2), 0, 1)).astype(jnp.int32)

    def part_of(value, who):
        return lax.dynamic_slice_in_dim(value, who * rows, rows, value.ndim - 2)

    sums = part_of(attn_partial[:, 0], y).astype(jnp.float32)
    for step in range(1, NY):
        piece = part_of(attn_partial[:, 0], (y + step) % NY)
        arrival = turn(piece, "y", NY, step)
        first_arrival = arrival if step == 1 else first_arrival
        sums = sums + arrival.astype(jnp.float32)
    stream = (part_of(residual, y).astype(jnp.float32) + sums).astype(jnp.bfloat16)
    normed = normalize(stream, norm_gain)

    def give(value):
        return lax.dynamic_index_in_dim(value, 1 - keep, 0, keepdims=False)

    kept = (w_gate, w_up, w_down)
    got_up = swap(tie(jnp.stack([give(w_gate), give(w_up)]), first_arrival))
    got_down = swap(tie(give(w_down), got_up))
    got = (got_up, got_down)

    left, digits = part_of(gate_weights, y), []
    for _ in range(3):
        digits.append(left.astype(jnp.bfloat16))
        left = left - digits[-1].astype(jnp.float32)
    fields = [part_of(expert_ids, y).astype(jnp.bfloat16), *digits]
    fields.append(jnp.zeros((micros, rows, LANES - 4 * top), jnp.bfloat16))
    sent = jnp.concatenate([normed, *fields], axis=-1)
    both = jnp.concatenate([sent, cores(sent)], axis=1)
    near, next_near = along(both, 1), along(both, 2)
    line = [sent, near, next_near, along(next_near, 1), along(next_near[:, :rows], 2)]
    line = tie(jnp.concatenate(line, axis=1), got_up)
    across = cores(line)

    arrivals, mixings = [], []
    for m in range(micros):
        tokens = jnp.concatenate([line[m], across[m]], axis=0)
        fields = tokens[:, width:].astype(jnp.float32)
        gates = fields[:, top : 2 * top] + fields[:, 2 * top : 3 * top] + fields[:, 3 * top : 4 * top]
        chooser, *mixing = tables(fields[:, :top].astype(jnp.int32), gates, rows, z, x, g, keep)
        mixings.append(mixing)
        routed = jnp.einsum("ts,td->sd", chooser, tokens[:, :width], preferred_element_type=jnp.float32)
        routed = routed.astype(jnp.bfloat16).reshape(NX, -1, width)
        arrived = [routed[step] if step == 0 else turn(routed[step], "x", NX, step) for step in range(NX)]
        arrivals.append(jnp.stack(arrived))

    results = []
    last = None
    for m in range(micros):
        arrived = arrivals[m]
        half = arrived.shape[1] // 2
        stay = arrived[:, :half].reshape(-1, width)
        leave = arrived[:, half:].reshape(-1, width)
        if m == 0:
            leave = tie(leave, got_down)
        came = swap(leave)
        pair_stay, pair_came = pair(stay), pair(came)
        mine_stay, mine_came = experts(keep, stay, came, kept, got, stay if last is None else last)
        pair_stay, pair_came = experts(keep, pair_stay, pair_came, kept, got, mine_came)
        last = pair_came
        back_came = pair(pair_came)
        if m > 0:
            back_came = tie(back_came, away)
        away = (mine_came.astype(jnp.float32) + back_came.astype(jnp.float32)).astype(jnp.bfloat16)
        away = swap(away)
        here = (mine_stay.astype(jnp.float32) + pair(pair_stay).astype(jnp.float32)).astype(jnp.bfloat16)
        answers = []
        for step in range(NX):
            span = slice(step * half, (step + 1) * half)
            piece = jnp.concatenate([here[span], away[span]], axis=0)
            answers.append(piece if step == 0 else turn(piece, "x", NX, -step))
        ordered = jnp.concatenate(answers, axis=0)
        if m > 0:
            ordered = tie(ordered, results[-1])
        total = jnp.dot(mixings[m][0], ordered, preferred_element_type=jnp.float32) + jnp.dot(
            mixings[m][1], ordered, preferred_element_type=jnp.float32
        )
        count = NZ * rows
        other = cores(total[count:].astype(jnp.bfloat16))
        back = (total[:count] + other.astype(jnp.float32)).astype(jnp.bfloat16)
        layer = stream[m].astype(jnp.float32) + back[:rows].astype(jnp.float32)
        beside = jnp.zeros((rows, width), jnp.float32)
        for step in range(1, NZ // 2):
            first = (2 * step - 1) * rows
            came = along(back[first : first + 2 * rows], -step).astype(jnp.float32)
            layer, beside = layer + came[:rows], beside + came[rows:]
        layer = layer + along(back[count - rows :], NZ // 2).astype(jnp.float32)
        layer = layer + cores(beside.astype(jnp.bfloat16)).astype(jnp.float32)
        results.append(layer.astype(jnp.bfloat16))
    return jnp.stack(results)


def solution(mesh):
    fine = Mesh(mesh.devices.reshape(NZ, NX, NY, NG), ("z", "x", "y", "g"))
    owners = ("z", "x", "g")
    return jax.shard_map(
        per_device,
        mesh=fine,
        in_specs=(
            P(None, "y", owners, None),
            P(None, owners, None),
            P(),
            P(None, owners, None),
            P(None, owners, None),
            P(owners, None, "y"),
            P(owners, None, "y"),
            P(owners, "y", None),
        ),
        out_specs=P(None, ("z", "x", "g", "y"), None),
        check_vma=False,
    )
```

```python
import jax
import jax.numpy as jnp
from jax import lax
from jax.experimental import pallas as pl
from jax.experimental.pallas import tpu as pltpu
from jax.sharding import Mesh, PartitionSpec as P

NZ, NX, NY, NG = 8, 4, 4, 2
SLOTS = 2
CHUNKS = 2
LANES = 128


def normalize(stream, norm_gain):
    values = stream.astype(jnp.float32)
    factor = lax.rsqrt(jnp.mean(values * values, axis=-1, keepdims=True) + 1e-06)
    return (values * factor * norm_gain).astype(jnp.bfloat16)


def yg_perm(first, second):
    return [(y * NG + g, (first(y) if g == 0 else second(y)) * NG + g) for y in range(NY) for g in range(NG)]


def mirror(y):
    return NY - 1 - y


def flip(y):
    return y ^ 1


SWAP = yg_perm(mirror, flip)
PAIR = yg_perm(flip, mirror)
CORES = [(0, 1), (1, 0)]


def swap(value):
    return lax.ppermute(value, ("y", "g"), SWAP)


def pair(value):
    return lax.ppermute(value, ("y", "g"), PAIR)


def cores(value):
    return lax.ppermute(value, "g", CORES)


def turn(value, axis, size, step):
    return lax.ppermute(value, axis, [(i, (i + step) % size) for i in range(size)])


def along(value, step):
    pairs = [(z * NG + g, (z + (step if g == 0 else -step)) % NZ * NG + g) for z in range(NZ) for g in range(NG)]
    return lax.ppermute(value, ("z", "g"), pairs)


def tables(ids, gates, rows, z, x, g, keep):
    tokens, top = ids.shape
    blocks = tokens // rows
    slots = NX * 2 * blocks * SLOTS
    slot = jnp.arange(slots, dtype=jnp.int32)[None, :]
    token = jnp.arange(tokens, dtype=jnp.int32)[:, None]
    which = slot // (blocks * SLOTS)
    local = jnp.where(which % 2 == 0, keep, 1 - keep)
    expert = (z * NX + (x + which // 2) % NX) * (2 * NG) + g * 2 + local
    same_block = (slot // SLOTS) % blocks == token // rows
    member = jnp.zeros((tokens, slots), jnp.float32)
    weight = jnp.zeros((tokens, slots), jnp.float32)
    for k in range(top):
        hit = (ids[:, k : k + 1] == expert) & same_block
        member = jnp.where(hit, 1.0, member)
        weight = jnp.where(hit, gates[:, k : k + 1], weight)
    other = jnp.arange(tokens, dtype=jnp.int32)[None, :]
    before = ((other < token) & (other // rows == token // rows)).astype(jnp.bfloat16)
    earlier = jnp.dot(before, member.astype(jnp.bfloat16), preferred_element_type=jnp.float32)
    taken = (member > 0.5) & (earlier.astype(jnp.int32) == slot % SLOTS)
    weight = jnp.where(taken, weight, 0.0)
    coarse = weight.astype(jnp.bfloat16)
    fine = (weight - coarse.astype(jnp.float32)).astype(jnp.bfloat16)
    return taken.astype(jnp.bfloat16), coarse, fine


def expert_kernel(keep_ref, a_ref, b_ref, gk, uk, got_ref, dk, dg, after_ref, oa_ref, ob_ref, act):
    del after_ref
    step = pl.program_id(0)
    half = a_ref.shape[0]
    hid = gk.shape[1]

    @pl.when(step == 0)
    def _():
        rows = jnp.concatenate([a_ref[...], b_ref[...]], axis=0)
        for n, (up_to, by) in enumerate(((gk, uk), (got_ref.at[0], got_ref.at[1]))):
            gate = jnp.dot(rows, up_to[...], preferred_element_type=jnp.float32)
            upper = jnp.dot(rows, by[...], preferred_element_type=jnp.float32)
            active = gate / (1.0 + jnp.exp(-gate)) * upper
            act[:, n * hid : (n + 1) * hid] = active.astype(jnp.bfloat16)

    @pl.when(step > 0)
    def _():
        out = jnp.dot(act[:, :hid], dk[...], preferred_element_type=jnp.float32)
        out += jnp.dot(act[:, hid:], dg[...], preferred_element_type=jnp.float32)
        out = out.astype(jnp.bfloat16)
        oa_ref[...] = out[:half]
        ob_ref[...] = out[half:]


def experts(keep, a, b, kept, got, after):
    half, width = a.shape
    hid = got[1].shape[0]
    wide = width // CHUNKS

    def late(i):
        return jnp.maximum(i - 1, 0)

    rows_spec = pl.BlockSpec((half, width), lambda i, keep: (0, 0))
    kept_up = pl.BlockSpec((None, width, hid), lambda i, keep: (keep[0], 0, 0))
    got_up = pl.BlockSpec((2, width, hid), lambda i, keep: (0, 0, 0))
    kept_down = pl.BlockSpec((None, hid, wide), lambda i, keep: (keep[0], 0, late(i)))
    got_down = pl.BlockSpec((hid, wide), lambda i, keep: (0, late(i)))
    out_spec = pl.BlockSpec((half, wide), lambda i, keep: (0, late(i)))
    return pl.pallas_call(
        expert_kernel,
        out_shape=[jax.ShapeDtypeStruct((half, width), jnp.bfloat16)] * 2,
        grid_spec=pltpu.PrefetchScalarGridSpec(
            num_scalar_prefetch=1,
            grid=(1 + CHUNKS,),
            in_specs=[rows_spec, rows_spec, kept_up, kept_up, got_up, kept_down, got_down, pl.BlockSpec(memory_space=pl.ANY)],
            out_specs=[out_spec, out_spec],
            scratch_shapes=[pltpu.VMEM((2 * half, 2 * hid), jnp.bfloat16)],
        ),
        compiler_params=pltpu.CompilerParams(
            dimension_semantics=("arbitrary",), vmem_limit_bytes=28 * 1024 * 1024
        ),
        cost_estimate=pl.CostEstimate(
            flops=2 * 2 * half * width * hid * 6,
            bytes_accessed=2 * (6 * hid * width + 4 * half * width),
            transcendentals=2 * half * 2 * hid,
        ),
    )(keep.reshape(1), a, b, kept[0], kept[1], got[0], kept[2], got[1], after)


def tie_kernel(value_ref, after_ref, out_ref):
    del value_ref, after_ref, out_ref


def tie(value, after):
    return pl.pallas_call(
        tie_kernel,
        out_shape=jax.ShapeDtypeStruct(value.shape, value.dtype),
        in_specs=[pl.BlockSpec(memory_space=pl.ANY)] * 2,
        out_specs=pl.BlockSpec(memory_space=pl.ANY),
        input_output_aliases={0: 0},
        cost_estimate=pl.CostEstimate(flops=0, bytes_accessed=0, transcendentals=0),
    )(value, after)


def per_device(attn_partial, residual, norm_gain, expert_ids, gate_weights, w_gate, w_up, w_down):
    micros = residual.shape[0]
    rows = residual.shape[1] // NY
    width = residual.shape[2]
    top = expert_ids.shape[-1]
    z, x, y, g = (lax.axis_index(name) for name in ("z", "x", "y", "g"))
    keep = jnp.where(g == 0, y // 2, jnp.where((y == 1) | (y == 2), 0, 1)).astype(jnp.int32)

    def part_of(value, who):
        return lax.dynamic_slice_in_dim(value, who * rows, rows, value.ndim - 2)

    sums = part_of(attn_partial[:, 0], y).astype(jnp.float32)
    for step in range(1, NY):
        piece = part_of(attn_partial[:, 0], (y + step) % NY)
        arrival = turn(piece, "y", NY, step)
        first_arrival = arrival if step == 1 else first_arrival
        sums = sums + arrival.astype(jnp.float32)
    stream = (part_of(residual, y).astype(jnp.float32) + sums).astype(jnp.bfloat16)
    normed = normalize(stream, norm_gain)

    def give(value):
        return lax.dynamic_index_in_dim(value, 1 - keep, 0, keepdims=False)

    kept = (w_gate, w_up, w_down)
    got_up = swap(tie(jnp.stack([give(w_gate), give(w_up)]), first_arrival))
    got_down = swap(tie(give(w_down), got_up))
    got = (got_up, got_down)

    left, digits = part_of(gate_weights, y), []
    for _ in range(3):
        digits.append(left.astype(jnp.bfloat16))
        left = left - digits[-1].astype(jnp.float32)
    fields = [part_of(expert_ids, y).astype(jnp.bfloat16), *digits]
    fields.append(jnp.zeros((micros, rows, LANES - 4 * top), jnp.bfloat16))
    sent = jnp.concatenate([normed, *fields], axis=-1)
    both = jnp.concatenate([sent, cores(sent)], axis=1)
    near, next_near = along(both, 1), along(both, 2)
    line = [sent, near, next_near, along(next_near, 1), along(next_near[:, :rows], 2)]
    line = tie(jnp.concatenate(line, axis=1), got_up)
    across = cores(line)

    arrivals, mixings = [], []
    for m in range(micros):
        tokens = jnp.concatenate([line[m], across[m]], axis=0)
        fields = tokens[:, width:].astype(jnp.float32)
        gates = fields[:, top : 2 * top] + fields[:, 2 * top : 3 * top] + fields[:, 3 * top : 4 * top]
        chooser, *mixing = tables(fields[:, :top].astype(jnp.int32), gates, rows, z, x, g, keep)
        mixings.append(mixing)
        routed = jnp.einsum("ts,td->sd", chooser, tokens[:, :width], preferred_element_type=jnp.float32)
        routed = routed.astype(jnp.bfloat16).reshape(NX, -1, width)
        arrived = [routed[step] if step == 0 else turn(routed[step], "x", NX, step) for step in range(NX)]
        arrivals.append(jnp.stack(arrived))

    last = away = None
    heres, aways = [], []
    for m in range(micros):
        arrived = arrivals[m]
        half = arrived.shape[1] // 2
        stay = arrived[:, :half].reshape(-1, width)
        leave = arrived[:, half:].reshape(-1, width)
        if m == 0:
            leave = tie(leave, got_down)
        came = swap(leave)
        pair_stay, pair_came = pair(stay), pair(came)
        mine_stay, mine_came = experts(keep, stay, came, kept, got, stay if last is None else last)
        pair_stay, pair_came = experts(keep, pair_stay, pair_came, kept, got, mine_came)
        last = pair_came
        back_came = pair(pair_came)
        if m > 0:
            back_came = tie(back_came, away)
        away = (mine_came.astype(jnp.float32) + back_came.astype(jnp.float32)).astype(jnp.bfloat16)
        away = swap(away)
        aways.append(away)
        heres.append((mine_stay.astype(jnp.float32) + pair(pair_stay).astype(jnp.float32)).astype(jnp.bfloat16))

    results = []
    first_back = None
    for m in range(micros):
        here, away = heres[m], aways[m]
        half = here.shape[0] // NX
        answers = []
        for step in range(NX):
            span = slice(step * half, (step + 1) * half)
            piece = jnp.concatenate([here[span], away[span]], axis=0)
            answers.append(piece if step == 0 else turn(piece, "x", NX, -step))
        ordered = tie(jnp.concatenate(answers, axis=0), aways[-1] if m == 0 else first_back)
        total = jnp.dot(mixings[m][0], ordered, preferred_element_type=jnp.float32) + jnp.dot(
            mixings[m][1], ordered, preferred_element_type=jnp.float32
        )
        count = NZ * rows
        other = cores(total[count:].astype(jnp.bfloat16))
        sums_z = (total[:count] + other.astype(jnp.float32)).astype(jnp.bfloat16)
        layer = stream[m].astype(jnp.float32) + sums_z[:rows].astype(jnp.float32)
        beside = jnp.zeros((rows, width), jnp.float32)
        for step in range(1, NZ // 2):
            first = (2 * step - 1) * rows
            came = along(sums_z[first : first + 2 * rows], -step)
            first_back = came if first_back is None else first_back
            came = came.astype(jnp.float32)
            layer, beside = layer + came[:rows], beside + came[rows:]
        layer = layer + along(sums_z[count - rows :], NZ // 2).astype(jnp.float32)
        layer = layer + cores(beside.astype(jnp.bfloat16)).astype(jnp.float32)
        results.append(layer.astype(jnp.bfloat16))
    return jnp.stack(results)


def solution(mesh):
    fine = Mesh(mesh.devices.reshape(NZ, NX, NY, NG), ("z", "x", "y", "g"))
    owners = ("z", "x", "g")
    return jax.shard_map(
        per_device,
        mesh=fine,
        in_specs=(
            P(None, "y", owners, None),
            P(None, owners, None),
            P(),
            P(None, owners, None),
            P(None, owners, None),
            P(owners, None, "y"),
            P(owners, None, "y"),
            P(owners, "y", None),
        ),
        out_specs=P(None, ("z", "x", "g", "y"), None),
        check_vma=False,
    )
```

```python
import jax
import jax.numpy as jnp
from jax import lax
from jax.experimental import pallas as pl
from jax.experimental.pallas import tpu as pltpu
from jax.sharding import Mesh, PartitionSpec as P

NZ, NX, NY, NG = 8, 4, 4, 2
SLOTS = 2
CHUNKS = 2
LANES = 128


def normalize(stream, norm_gain):
    values = stream.astype(jnp.float32)
    factor = lax.rsqrt(jnp.mean(values * values, axis=-1, keepdims=True) + 1e-06)
    return (values * factor * norm_gain).astype(jnp.bfloat16)


def yg_perm(first, second):
    return [(y * NG + g, (first(y) if g == 0 else second(y)) * NG + g) for y in range(NY) for g in range(NG)]


def mirror(y):
    return NY - 1 - y


def flip(y):
    return y ^ 1


SWAP = yg_perm(mirror, flip)
PAIR = yg_perm(flip, mirror)
CORES = [(0, 1), (1, 0)]


def swap(value):
    return lax.ppermute(value, ("y", "g"), SWAP)


def pair(value):
    return lax.ppermute(value, ("y", "g"), PAIR)


def cores(value):
    return lax.ppermute(value, "g", CORES)


def turn(value, axis, size, step):
    return lax.ppermute(value, axis, [(i, (i + step) % size) for i in range(size)])


def along(value, step):
    pairs = [(z * NG + g, (z + (step if g == 0 else -step)) % NZ * NG + g) for z in range(NZ) for g in range(NG)]
    return lax.ppermute(value, ("z", "g"), pairs)


def tables(ids, gates, rows, z, x, g, keep):
    tokens, top = ids.shape
    blocks = tokens // rows
    slots = NX * 2 * blocks * SLOTS
    slot = jnp.arange(slots, dtype=jnp.int32)[None, :]
    token = jnp.arange(tokens, dtype=jnp.int32)[:, None]
    which = slot // (blocks * SLOTS)
    local = jnp.where(which % 2 == 0, keep, 1 - keep)
    expert = (z * NX + (x + which // 2) % NX) * (2 * NG) + g * 2 + local
    same_block = (slot // SLOTS) % blocks == token // rows
    member = jnp.zeros((tokens, slots), jnp.float32)
    weight = jnp.zeros((tokens, slots), jnp.float32)
    for k in range(top):
        hit = (ids[:, k : k + 1] == expert) & same_block
        member = jnp.where(hit, 1.0, member)
        weight = jnp.where(hit, gates[:, k : k + 1], weight)
    other = jnp.arange(tokens, dtype=jnp.int32)[None, :]
    before = ((other < token) & (other // rows == token // rows)).astype(jnp.bfloat16)
    earlier = jnp.dot(before, member.astype(jnp.bfloat16), preferred_element_type=jnp.float32)
    taken = (member > 0.5) & (earlier.astype(jnp.int32) == slot % SLOTS)
    weight = jnp.where(taken, weight, 0.0)
    coarse = weight.astype(jnp.bfloat16)
    fine = (weight - coarse.astype(jnp.float32)).astype(jnp.bfloat16)
    return taken.astype(jnp.bfloat16), coarse, fine


def expert_kernel(keep_ref, a_ref, b_ref, gk, uk, got_ref, dk, dg, after_ref, oa_ref, ob_ref, act):
    del after_ref
    step = pl.program_id(0)
    half = a_ref.shape[0]
    hid = gk.shape[1]

    @pl.when(step == 0)
    def _():
        rows = jnp.concatenate([a_ref[...], b_ref[...]], axis=0)
        for n, (up_to, by) in enumerate(((gk, uk), (got_ref.at[0], got_ref.at[1]))):
            gate = jnp.dot(rows, up_to[...], preferred_element_type=jnp.float32)
            upper = jnp.dot(rows, by[...], preferred_element_type=jnp.float32)
            active = gate / (1.0 + jnp.exp(-gate)) * upper
            act[:, n * hid : (n + 1) * hid] = active.astype(jnp.bfloat16)

    @pl.when(step > 0)
    def _():
        out = jnp.dot(act[:, :hid], dk[...], preferred_element_type=jnp.float32)
        out += jnp.dot(act[:, hid:], dg[...], preferred_element_type=jnp.float32)
        out = out.astype(jnp.bfloat16)
        oa_ref[...] = out[:half]
        ob_ref[...] = out[half:]


def experts(keep, a, b, kept, got, after):
    half, width = a.shape
    hid = got[1].shape[0]
    wide = width // CHUNKS

    def late(i):
        return jnp.maximum(i - 1, 0)

    rows_spec = pl.BlockSpec((half, width), lambda i, keep: (0, 0))
    kept_up = pl.BlockSpec((None, width, hid), lambda i, keep: (keep[0], 0, 0))
    got_up = pl.BlockSpec((2, width, hid), lambda i, keep: (0, 0, 0))
    kept_down = pl.BlockSpec((None, hid, wide), lambda i, keep: (keep[0], 0, late(i)))
    got_down = pl.BlockSpec((hid, wide), lambda i, keep: (0, late(i)))
    out_spec = pl.BlockSpec((half, wide), lambda i, keep: (0, late(i)))
    return pl.pallas_call(
        expert_kernel,
        out_shape=[jax.ShapeDtypeStruct((half, width), jnp.bfloat16)] * 2,
        grid_spec=pltpu.PrefetchScalarGridSpec(
            num_scalar_prefetch=1,
            grid=(1 + CHUNKS,),
            in_specs=[rows_spec, rows_spec, kept_up, kept_up, got_up, kept_down, got_down, pl.BlockSpec(memory_space=pl.ANY)],
            out_specs=[out_spec, out_spec],
            scratch_shapes=[pltpu.VMEM((2 * half, 2 * hid), jnp.bfloat16)],
        ),
        compiler_params=pltpu.CompilerParams(
            dimension_semantics=("arbitrary",), vmem_limit_bytes=28 * 1024 * 1024
        ),
        cost_estimate=pl.CostEstimate(
            flops=2 * 2 * half * width * hid * 6,
            bytes_accessed=2 * (6 * hid * width + 4 * half * width),
            transcendentals=2 * half * 2 * hid,
        ),
    )(keep.reshape(1), a, b, kept[0], kept[1], got[0], kept[2], got[1], after)


def tie_kernel(value_ref, after_ref, out_ref):
    del value_ref, after_ref, out_ref


def tie(value, after):
    return pl.pallas_call(
        tie_kernel,
        out_shape=jax.ShapeDtypeStruct(value.shape, value.dtype),
        in_specs=[pl.BlockSpec(memory_space=pl.ANY)] * 2,
        out_specs=pl.BlockSpec(memory_space=pl.ANY),
        input_output_aliases={0: 0},
        cost_estimate=pl.CostEstimate(flops=0, bytes_accessed=0, transcendentals=0),
    )(value, after)


def per_device(attn_partial, residual, norm_gain, expert_ids, gate_weights, w_gate, w_up, w_down):
    micros = residual.shape[0]
    rows = residual.shape[1] // NY
    width = residual.shape[2]
    top = expert_ids.shape[-1]
    z, x, y, g = (lax.axis_index(name) for name in ("z", "x", "y", "g"))
    keep = jnp.where(g == 0, y // 2, jnp.where((y == 1) | (y == 2), 0, 1)).astype(jnp.int32)

    def part_of(value, who):
        return lax.dynamic_slice_in_dim(value, who * rows, rows, value.ndim - 2)

    sums = part_of(attn_partial[:, 0], y).astype(jnp.float32)
    for step in range(1, NY):
        piece = part_of(attn_partial[:, 0], (y + step) % NY)
        arrival = turn(piece, "y", NY, step)
        first_arrival = arrival if step == 1 else first_arrival
        sums = sums + arrival.astype(jnp.float32)
    stream = (part_of(residual, y).astype(jnp.float32) + sums).astype(jnp.bfloat16)
    normed = normalize(stream, norm_gain)

    def give(value):
        return lax.dynamic_index_in_dim(value, 1 - keep, 0, keepdims=False)

    kept = (w_gate, w_up, w_down)
    got_up = swap(tie(jnp.stack([give(w_gate), give(w_up)]), first_arrival))
    got_down = swap(tie(give(w_down), got_up))
    got = (got_up, got_down)

    left, digits = part_of(gate_weights, y), []
    for _ in range(3):
        digits.append(left.astype(jnp.bfloat16))
        left = left - digits[-1].astype(jnp.float32)
    fields = [part_of(expert_ids, y).astype(jnp.bfloat16), *digits]
    fields.append(jnp.zeros((micros, rows, LANES - 4 * top), jnp.bfloat16))
    sent = jnp.concatenate([normed, *fields], axis=-1)
    both = jnp.concatenate([sent, cores(sent)], axis=1)
    near, next_near = along(both, 1), along(both, 2)
    line = [sent, near, next_near, along(next_near, 1), along(next_near[:, :rows], 2)]
    line = tie(jnp.concatenate(line, axis=1), got_up)
    across = cores(line)

    arrivals, mixings = [], []
    for m in range(micros):
        tokens = jnp.concatenate([line[m], across[m]], axis=0)
        fields = tokens[:, width:].astype(jnp.float32)
        gates = fields[:, top : 2 * top] + fields[:, 2 * top : 3 * top] + fields[:, 3 * top : 4 * top]
        chooser, *mixing = tables(fields[:, :top].astype(jnp.int32), gates, rows, z, x, g, keep)
        mixings.append(mixing)
        routed = jnp.einsum("ts,td->sd", chooser, tokens[:, :width], preferred_element_type=jnp.float32)
        routed = routed.astype(jnp.bfloat16).reshape(NX, -1, width)
        arrived = [routed[step] if step == 0 else turn(routed[step], "x", NX, step) for step in range(NX)]
        arrivals.append(jnp.stack(arrived))

    results = []
    last = None
    for m in range(micros):
        arrived = arrivals[m]
        half = arrived.shape[1] // 2
        stay = arrived[:, :half].reshape(-1, width)
        leave = arrived[:, half:].reshape(-1, width)
        if m == 0:
            leave = tie(leave, got_down)
        came = swap(leave)
        pair_stay, pair_came = pair(stay), pair(came)
        mine_stay, mine_came = experts(keep, stay, came, kept, got, stay if last is None else last)
        pair_stay, pair_came = experts(keep, pair_stay, pair_came, kept, got, mine_came)
        last = pair_came
        away = (mine_came.astype(jnp.float32) + pair(pair_came).astype(jnp.float32)).astype(jnp.bfloat16)
        away = swap(away)
        here = (mine_stay.astype(jnp.float32) + pair(pair_stay).astype(jnp.float32)).astype(jnp.bfloat16)
        answers = []
        for step in range(NX):
            span = slice(step * half, (step + 1) * half)
            piece = jnp.concatenate([here[span], away[span]], axis=0)
            answers.append(piece if step == 0 else turn(piece, "x", NX, -step))
        ordered = jnp.concatenate(answers, axis=0)
        if m > 0:
            ordered = tie(ordered, results[-1])
        total = jnp.dot(mixings[m][0], ordered, preferred_element_type=jnp.float32) + jnp.dot(
            mixings[m][1], ordered, preferred_element_type=jnp.float32
        )
        count = NZ * rows
        other = cores(total[count:].astype(jnp.bfloat16))
        back = (total[:count] + other.astype(jnp.float32)).astype(jnp.bfloat16)
        layer = stream[m].astype(jnp.float32) + back[:rows].astype(jnp.float32)
        beside = jnp.zeros((rows, width), jnp.float32)
        for step in range(1, NZ // 2):
            first = (2 * step - 1) * rows
            came = along(back[first : first + 2 * rows], -step).astype(jnp.float32)
            layer, beside = layer + came[:rows], beside + came[rows:]
        layer = layer + along(back[count - rows :], NZ // 2).astype(jnp.float32)
        layer = layer + cores(beside.astype(jnp.bfloat16)).astype(jnp.float32)
        results.append(layer.astype(jnp.bfloat16))
    return jnp.stack(results)


def solution(mesh):
    fine = Mesh(mesh.devices.reshape(NZ, NX, NY, NG), ("z", "x", "y", "g"))
    owners = ("z", "x", "g")
    return jax.shard_map(
        per_device,
        mesh=fine,
        in_specs=(
            P(None, "y", owners, None),
            P(None, owners, None),
            P(),
            P(None, owners, None),
            P(None, owners, None),
            P(owners, None, "y"),
            P(owners, None, "y"),
            P(owners, "y", None),
        ),
        out_specs=P(None, ("z", "x", "g", "y"), None),
        check_vma=False,
    )
```
